32 devices in a mesh: dp: 8 (over y, x, core), tensor: 4 (over z).
Axes of the slice: x: 2, y: 2, z: 4, core: 2. Of those that a mesh axis runs over, the one named last changes fastest.
Arguments:
- activations: bfloat16 [4096, 4096], P(('dp', 'tensor')), may hold values from -6 to 6
- value_weight: bfloat16 [4096, 512], P('tensor'), may hold values from -0.09375 to 0.09375
- value_cotangent: bfloat16 [4096, 512], P(('dp', 'tensor')), may hold values from -6 to 6
Outputs:
- value_proj: bfloat16 [4096, 512], P(('dp', 'tensor'))
- input_grad: bfloat16 [4096, 4096], P(('dp', 'tensor'))
- weight_grad: float32 [4096, 512], P(('tensor', 'dp'))
The draws below stay inside these ranges and needn't reach their ends.
All inputs are finite; a program needn't handle non-finite values.
Results may differ from the reference program's by a relative error of at most 0.001.
Values may be sent and summed in bfloat16 or wider, within the bound.
No kernel may reach another device: no remote copies, remote signals or barrier semaphores. Data moves between devices by JAX's collectives and lax.ppermute only.
A program may use at most 64 MiB of HBM per device.

```python
import jax
import jax.numpy as jnp

D = 4096
VDIM = 512
TOKENS = 4096


def with_spikes(result, stream_key, source, target, blocks, factor):
    owner, partner = [(jnp.arange(result.shape[dim]) // (result.shape[dim] // blocks)).reshape([-1 if axis == dim else 1 for axis in range(result.ndim)]) for dim in (source, target)]
    chosen = jax.random.permutation(stream_key, blocks)[partner]
    strong = (owner == chosen) | (owner == (partner + blocks // 2) % blocks)
    return jnp.where(strong, factor * result, result)


def block_scale(stream_key, shape, split, low, top_value):
    def one(dim, parts):
        steps = jax.random.uniform(jax.random.fold_in(jax.random.fold_in(stream_key, 6), dim), (parts,), jnp.float32, low / len(split), top_value / len(split))
        return jnp.repeat(jnp.exp(steps), shape[dim] // parts).reshape((-1,) + (1,) * (len(shape) - dim - 1))

    gain = one(*split[0])
    for cut in split[1:]:
        gain = gain * one(*cut)
    return gain


def centred(key, shape, scale, most, cuts=(), held_as=jnp.bfloat16):
    drawn = scale * jax.random.normal(key, shape, jnp.float32)
    if cuts:
        drawn = drawn * block_scale(key, shape, cuts, -0.22, 0.18)
    return jnp.clip(drawn, -most, most).astype(held_as)


def gaussian_with(own_key, dims, scale, bound, split, heavy, dtype=jnp.bfloat16):
    result = scale * jax.random.normal(own_key, dims, jnp.float32)
    if split:
        result = result * block_scale(own_key, dims, split, -0.22, 0.18)
    return jnp.clip(with_spikes(result, jax.random.fold_in(own_key, 3), *heavy), -bound, bound).astype(dtype)


def setup_inputs(seed: int = 0) -> dict:
    streams_of = jax.random.split(jax.random.key(seed), 4)
    return {
        "activations": gaussian_with(streams_of[0], (TOKENS, D), 1.0, 6.0, ((0, 32),), (0, 1, 32, 2.75)),
        "value_weight": centred(streams_of[1], (D, VDIM), D ** -0.5, 0.09375, ((0, 4),)),
        "value_cotangent": centred(streams_of[2], (TOKENS, VDIM), 1.0, 6.0, ((0, 32),)),
    }


def reference(activations, value_weight, value_cotangent):
    value_proj = jnp.dot(activations, value_weight, preferred_element_type=jnp.float32).astype(jnp.bfloat16)
    input_grad = jnp.dot(value_cotangent, value_weight.T, preferred_element_type=jnp.float32).astype(jnp.bfloat16)
    total = jnp.dot(activations.T, value_cotangent, preferred_element_type=jnp.float32)
    weight_grad = total / jnp.sqrt(jnp.float32(TOKENS))
    return (value_proj, input_grad, weight_grad)
```

```python
import functools

import jax
import jax.numpy as jnp
from jax import lax
from jax.experimental import pallas as pl
from jax.experimental.pallas import tpu as pltpu
from jax.sharding import PartitionSpec as P

LANES = 128
AXES = ("dp", "tensor")


def contract(a, b, dim_a, dim_b):
    return lax.dot_general(a, b, (((dim_a,), (dim_b,)), ((), ())), preferred_element_type=jnp.float32)


def gathered_form(activations, value_weight, value_cotangent):
    tok_rows = activations.shape[0]
    full_weight = lax.all_gather(value_weight, "tensor", axis=0, tiled=True)
    value_proj = contract(activations, full_weight, 1, 0).astype(jnp.bfloat16)
    input_grad = contract(value_cotangent, full_weight, 1, 1).astype(jnp.bfloat16)
    own_columns = lax.all_to_all(activations, "tensor", split_axis=1, concat_axis=0, tiled=True)
    group_term = contract(own_columns, lax.all_gather(value_cotangent, "tensor", axis=0, tiled=True), 0, 0)
    summed = lax.psum_scatter(group_term, "dp", scatter_dimension=0, tiled=True)
    total_tokens = tok_rows * lax.axis_size("dp") * lax.axis_size("tensor")
    return value_proj, input_grad, summed / jnp.sqrt(jnp.float32(total_tokens))


def exchange(x, n_dp, n_tensor, dp_xor, tensor_xor):
    pairs = [(d * n_tensor + t, (d ^ dp_xor) * n_tensor + (t ^ tensor_xor)) for d in range(n_dp) for t in range(n_tensor)]
    return lax.ppermute(x, AXES, pairs)


def kernel_call(body, out_shapes, args, in_specs=None, name=None, flops=0):
    size = sum(a.size * a.dtype.itemsize for a in args) + sum(o.size * o.dtype.itemsize for o in out_shapes)
    whole = pl.BlockSpec(memory_space=pltpu.VMEM)
    return pl.pallas_call(
        body,
        out_shape=out_shapes,
        in_specs=in_specs or [whole] * len(args),
        out_specs=[whole] * len(out_shapes),
        compiler_params=pltpu.CompilerParams(vmem_limit_bytes=32 * 1024 * 1024),
        cost_estimate=pl.CostEstimate(flops=flops, bytes_accessed=size, transcendentals=0),
        name=name,
    )(*args)


def paired_form(n_dp, n_tensor, activations, value_weight, value_cotangent):
    tok, depth = activations.shape
    vdim = value_cotangent.shape[1]
    blk = depth // (n_dp * n_tensor)
    chips = n_dp // 2
    swap = functools.partial(exchange, n_dp=n_dp, n_tensor=n_tensor)
    bf16, f32 = jnp.bfloat16, jnp.float32

    def column(quarter, chip, core=0):
        return pl.multiple_of(((quarter * chips + chip) * 2 + core) * blk, LANES)

    def place():
        d = lax.axis_index("dp")
        return d // 2, d % 2, lax.axis_index("tensor")

    far = list(range(n_tensor // 2, n_tensor))
    near = list(range(n_tensor // 2))

    def pack(js, with_cot):
        def body(act, cot, *outs):
            p, _, t = place()
            for q, out in enumerate(outs, 1):
                for i, j in enumerate(js):
                    out[:, i * 2 * blk : (i + 1) * 2 * blk] = act[:, pl.ds(column(t ^ j, p ^ q), 2 * blk)]
                if with_cot:
                    out[:, len(js) * 2 * blk :] = cot[...]

        width = len(js) * 2 * blk + (vdim if with_cot else 0)
        shapes = [jax.ShapeDtypeStruct((tok, width), bf16)] * (chips - 1)
        return kernel_call(body, shapes, [activations, value_cotangent], name="pack")

    def partial_sums(js, strips, cots):
        n = chips - 1

        def body(act, cot, *refs):
            strip_refs, cot_refs, (keep, send) = refs[:n], refs[n : 2 * n], refs[2 * n :]
            p, c, t = place()
            all_cots = jnp.concatenate([cot[...]] + [r[:, far_width:] for r in cot_refs], axis=0)
            for i, j in enumerate(js):
                for out, core in ((send, 1 - c), (keep, c)):
                    start = pl.multiple_of(i * 2 * blk + core * blk, LANES)
                    parts = [act[:, pl.ds(column(t ^ j, p, core), blk)]] + [r[:, pl.ds(start, blk)] for r in strip_refs]
                    out[i * blk : (i + 1) * blk, :] = contract(jnp.concatenate(parts, axis=0), all_cots, 0, 0)

        shape = jax.ShapeDtypeStruct((len(js) * blk, vdim), f32)
        flops = 4 * len(js) * blk * vdim * tok * chips
        return kernel_call(body, [shape, shape], [activations, value_cotangent, *strips, *cots], name="partial_sums", flops=flops)

    far_width = len(far) * 2 * blk

    own_slice = lax.dynamic_slice_in_dim(value_weight, lax.axis_index("dp") * blk, blk, 0)
    slices = [swap(own_slice, dp_xor=0, tensor_xor=j) for j in range(1, n_tensor)]
    far_got = [swap(x, dp_xor=2 * q, tensor_xor=0) for q, x in enumerate(pack(far, True), 1)]
    near_got = [swap(x, dp_xor=2 * q, tensor_xor=0) for q, x in enumerate(pack(near, False), 1)]
    mine = jnp.concatenate(slices, axis=0)
    weight_got = [mine] + [swap(mine, dp_xor=2 * q, tensor_xor=0) for q in range(1, chips)]
    weight_twin = [swap(x, dp_xor=1, tensor_xor=0) for x in weight_got]

    far_keep, far_send = partial_sums(far, far_got, far_got)
    far_sum = far_keep + swap(far_send, dp_xor=1, tensor_xor=0)
    terms = [swap(far_sum[i * blk : (i + 1) * blk], dp_xor=0, tensor_xor=j) for i, j in enumerate(far)]
    near_keep, near_send = partial_sums(near, near_got, far_got)
    near_sum = near_keep + swap(near_send, dp_xor=1, tensor_xor=0)
    terms += [swap(near_sum[i * blk : (i + 1) * blk], dp_xor=0, tensor_xor=j) for i, j in enumerate(near) if j]
    summed = near_sum[:blk]
    for term in terms:
        summed = summed + term
    weight_grad = summed / jnp.sqrt(f32(tok * n_dp * n_tensor))

    quarter = depth // n_tensor

    def quarter_body(act, cot, w, acc, grad):
        _, _, t = place()
        acc[...] = contract(act[:, pl.ds(pl.multiple_of(t * quarter, LANES), quarter)], w[...], 1, 0)
        grad[...] = contract(cot[...], w[...], 1, 1).astype(bf16)

    acc, quarter_grad = kernel_call(
        quarter_body,
        [jax.ShapeDtypeStruct((tok, vdim), f32), jax.ShapeDtypeStruct((tok, quarter), bf16)],
        [activations, value_cotangent, value_weight],
        name="own_quarter",
        flops=4 * tok * vdim * quarter,
    )

    def rest_body(act, cot, acc, quarter_grad, *refs):
        got, twin, (proj, grad) = refs[:chips], refs[chips : 2 * chips], refs[2 * chips :]
        p, c, t = place()
        grad[:, pl.ds(pl.multiple_of(t * quarter, LANES), quarter)] = quarter_grad[...]
        total = acc[...]
        for q in range(chips):
            for j in range(1, n_tensor):
                for ref, core in ((got[q], c), (twin[q], 1 - c)):
                    w = ref[(j - 1) * blk : j * blk, :]
                    cols = pl.ds(column(t ^ j, p ^ q, core), blk)
                    total += contract(act[:, cols], w, 1, 0)
                    grad[:, cols] = contract(cot[...], w, 1, 1).astype(bf16)
        proj[...] = total.astype(bf16)

    value_proj, input_grad = kernel_call(
        rest_body,
        [jax.ShapeDtypeStruct((tok, vdim), bf16), jax.ShapeDtypeStruct((tok, depth), bf16)],
        [activations, value_cotangent, acc, quarter_grad, *weight_got, *weight_twin],
        name="other_quarters",
        flops=4 * tok * vdim * (depth - quarter),
    )
    return value_proj, input_grad, weight_grad


def solution(mesh):
    n_dp, n_tensor = mesh.shape["dp"], mesh.shape["tensor"]

    def per_device(activations, value_weight, value_cotangent):
        tok, depth = activations.shape
        powers = all(n > 1 and n & (n - 1) == 0 for n in (n_dp, n_tensor))
        if powers and depth % (n_dp * n_tensor * LANES) == 0 and tok % LANES == 0:
            return paired_form(n_dp, n_tensor, activations, value_weight, value_cotangent)
        return gathered_form(activations, value_weight, value_cotangent)

    return jax.shard_map(
        per_device,
        mesh=mesh,
        in_specs=(P(AXES, None), P("tensor", None), P(AXES, None)),
        out_specs=(P(AXES, None), P(AXES, None), P(("tensor", "dp"), None)),
        check_vma=False,
    )
```

```python
import functools

import jax
import jax.numpy as jnp
from jax import lax
from jax.experimental import pallas as pl
from jax.experimental.pallas import tpu as pltpu
from jax.sharding import PartitionSpec as P

OPT = {'pf': 1, 's1_after3': 1, 'w_mode': 'whole', 'pack': 'vmem', 'pack_lim': 60, 's_mode': 'strip', 'z_mode': 'mix', 'e_mode': 'merged', 'sums_za': 1, 'sums_zb': 1, 'ca_zb': 1, 'mine_after': 0, 'st2_after': 1, 'e2_acc': 1, 'e2_s1': 1, 'e2_s2': 1, 'slice_after': 1, 'qtr_after': 'za', 'sums_qtr': 1, 'e1_s': 0, 'order': 'zs', 'c_pack': 0, 'c_slice': 0, 'c_zstack': 0, 'c_qtr': 0, 'c_sums1': 5, 'c_sums2': 0, 'c_join1': 0, 'c_join2': 0, 'c_joinf': 20, 'c_mine': 0, 'c_estack': 0, 'c_e2stack': 0, 'c_prod': 0, 'c_last': 0}
LANES = 128
PAD = 16
LOG2_E = 1.4426950408889634
TOP_POWER = 14.0
AXES = ("dp", "tensor")
VMEM_LIMIT = 32 * 1024 * 1024
PACK_LIMIT = 60 * 1024 * 1024


def contract(a, b, dim_a, dim_b):
    return lax.dot_general(a, b, (((dim_a,), (dim_b,)), ((), ())), preferred_element_type=jnp.float32)


def gathered_form(activations, value_weight, value_cotangent):
    tok_rows = activations.shape[0]
    full_weight = lax.all_gather(value_weight, "tensor", axis=0, tiled=True)
    value_proj = contract(activations, full_weight, 1, 0).astype(jnp.bfloat16)
    input_grad = contract(value_cotangent, full_weight, 1, 1).astype(jnp.bfloat16)
    own_columns = lax.all_to_all(activations, "tensor", split_axis=1, concat_axis=0, tiled=True)
    group_term = contract(own_columns, lax.all_gather(value_cotangent, "tensor", axis=0, tiled=True), 0, 0)
    summed = lax.psum_scatter(group_term, "dp", scatter_dimension=0, tiled=True)
    total_tokens = tok_rows * lax.axis_size("dp") * lax.axis_size("tensor")
    return value_proj, input_grad, summed / jnp.sqrt(jnp.float32(total_tokens))


def exchange(x, n_dp, n_tensor, dp_xor, tensor_xor):
    pairs = [(d * n_tensor + t, (d ^ dp_xor) * n_tensor + (t ^ tensor_xor)) for d in range(n_dp) for t in range(n_tensor)]
    return lax.ppermute(x, AXES, pairs)


def kernel_call(body, out_shapes, args, name, cost=0):
    whole = pl.BlockSpec(memory_space=pltpu.VMEM)
    return pl.pallas_call(
        body,
        out_shape=out_shapes,
        in_specs=[whole] * len(args),
        out_specs=[whole] * len(out_shapes),
        compiler_params=pltpu.CompilerParams(vmem_limit_bytes=VMEM_LIMIT),
        cost_estimate=pl.CostEstimate(flops=int(cost * 1.15e9), bytes_accessed=1024, transcendentals=0),
        name=name,
    )(*args)


def stack(parts, cost=0):
    parts = [p if isinstance(p, tuple) else (p, slice(0, p.shape[0])) for p in parts]

    def body(*refs):
        at = 0
        for ref, (_, cut) in zip(refs, parts):
            refs[-1][at : at + cut.stop - cut.start, :] = ref[cut, :]
            at += cut.stop - cut.start

    rows = sum(cut.stop - cut.start for _, cut in parts)
    out = jax.ShapeDtypeStruct((rows, parts[0][0].shape[1]), parts[0][0].dtype)
    return kernel_call(body, [out], [p for p, _ in parts], "stack", cost)[0]


def paired_form(n_dp, n_tensor, activations, value_weight, value_cotangent):
    tok, depth = activations.shape
    vdim = value_cotangent.shape[1]
    blk = depth // (n_dp * n_tensor)
    chips = n_dp // 2
    quarter = depth // n_tensor
    bf16, f32 = jnp.bfloat16, jnp.float32
    shape = jax.ShapeDtypeStruct
    barrier = lax.optimization_barrier

    def twin(x):
        return exchange(x, n_dp, n_tensor, 1, 0)

    def across(x, chip_xor):
        return exchange(x, n_dp, n_tensor, 2 * chip_xor, 0)

    def along(x, tensor_xor):
        return exchange(x, n_dp, n_tensor, 0, tensor_xor)

    def column(part, chip, core=0):
        return pl.multiple_of(((part * chips + chip) * 2 + core) * blk, LANES)

    def place():
        d = lax.axis_index("dp")
        return d // 2, d % 2, lax.axis_index("tensor")

    js = sorted(range(n_tensor), key=lambda j: (-j.bit_count(), -j)) if OPT["s_mode"] == "strip" else list(range(n_tensor - 1, -1, -1))
    width = n_tensor * 2 * blk

    def pack_body(act, cot, *outs):
        p, _, t = place()
        for q, out in enumerate(outs, 1):
            for i, j in enumerate(js):
                out[:, i * 2 * blk : (i + 1) * 2 * blk] = act[:, pl.ds(column(t ^ j, p ^ q), 2 * blk)]
            out[:, width:] = cot[...]

    def slice_body(weight, out):
        p, c, _ = place()
        out[...] = weight[pl.ds(pl.multiple_of((p * 2 + c) * blk, LANES), blk), :]

    if OPT["pack"] == "hbm":
        def pack_dma(act, cot, *refs):
            outs, sems = refs[:-1], refs[-1]
            p, _, t = place()
            pairs = []
            for q, out in enumerate(outs, 1):
                for i, j in enumerate(js):
                    pairs.append((act.at[:, pl.ds(column(t ^ j, p ^ q), 2 * blk)], out.at[:, i * 2 * blk : (i + 1) * 2 * blk]))
                pairs.append((cot, out.at[:, width:]))
            copies = [pltpu.make_async_copy(src, dst, sems.at[i]) for i, (src, dst) in enumerate(pairs)]
            for copy in copies:
                copy.start()
            for copy in copies:
                copy.wait()

        packs = pl.pallas_call(
            pack_dma,
            out_shape=[shape((tok, width + vdim), bf16)] * (chips - 1),
            in_specs=[pl.BlockSpec(memory_space=pltpu.HBM)] * 2,
            out_specs=[pl.BlockSpec(memory_space=pltpu.VMEM)] * (chips - 1),
            scratch_shapes=[pltpu.SemaphoreType.DMA(((chips - 1) * (n_tensor + 1),))],
            compiler_params=pltpu.CompilerParams(vmem_limit_bytes=int(OPT["pack_lim"] * 1024 * 1024)),
            cost_estimate=pl.CostEstimate(flops=int(OPT["c_pack"] * 1.15e9), bytes_accessed=1024, transcendentals=0),
            name="pack",
        )(activations, value_cotangent)
    else:
        packs = kernel_call(pack_body, [shape((tok, width + vdim), bf16)] * (chips - 1), [activations, value_cotangent], name="pack", cost=OPT["c_pack"])
    (own_slice,) = kernel_call(slice_body, [shape((blk, vdim), bf16)], [value_weight], name="own_slice", cost=OPT["c_slice"])
    if OPT["slice_after"]:
        own_slice, *packs = barrier((own_slice, *packs))
    got = [across(x, q) for q, x in enumerate(packs, 1)]

    if OPT["z_mode"] == "rec":
        held, slots = [own_slice], [0]
        bit = n_tensor // 2
        while bit:
            held.append(along(stack(held, OPT["c_zstack"]) if len(held) > 1 else held[0], bit))
            slots += [j ^ bit for j in slots]
            bit //= 2
        slots = slots[1:]
        held = held[1:]
    elif OPT["z_mode"] == "mix":
        slots = sorted(range(1, n_tensor), key=lambda j: (j.bit_count(), -j))
        by_slot = {0: own_slice}
        for j in slots:
            by_slot[j] = along(by_slot[j & (j - 1)], j & -j)
        held = [by_slot[j] for j in slots]
    else:
        slots = list(range(n_tensor - 1, 0, -1))
        held = [along(own_slice, j) for j in slots]

    def quarter_body(act, cot, w, acc, grad, columns, sem):
        _, _, t = place()
        own = pl.ds(pl.multiple_of(t * quarter, LANES), quarter)
        columns[...] = contract(cot[...], w[...], 1, 1).astype(bf16)
        copy = pltpu.make_async_copy(columns, grad.at[:, own], sem)
        copy.start()
        acc[...] = contract(act[:, own], w[...], 1, 0)
        copy.wait()

    whole, anywhere = pl.BlockSpec(memory_space=pltpu.VMEM), pl.BlockSpec(memory_space=pl.ANY)
    qw = value_weight
    if OPT["qtr_after"] == "pack":
        qw = barrier((value_weight, packs[0], got[0]))[0] if False else barrier((value_weight, own_slice))[0]
    elif OPT["qtr_after"] == "za":
        qw = barrier((value_weight, held[0]))[0]
    elif OPT["qtr_after"] == "a":
        qw = barrier((value_weight, got[0]))[0]
    acc, grad = pl.pallas_call(
        quarter_body,
        out_shape=[shape((tok, vdim), f32), shape((tok, depth), bf16)],
        in_specs=[whole] * 3,
        out_specs=[whole, anywhere],
        scratch_shapes=[pltpu.VMEM((tok, quarter), bf16), pltpu.SemaphoreType.DMA],
        compiler_params=pltpu.CompilerParams(vmem_limit_bytes=VMEM_LIMIT),
        cost_estimate=pl.CostEstimate(flops=int(OPT["c_qtr"] * 1.15e9), bytes_accessed=1024, transcendentals=0),
        name="own_quarter",
    )(activations, value_cotangent, value_weight)


    def sums_of(js_now, offset, cost):
        def body(act, cot, *refs):
            keep, send = refs[-2:]
            p, c, t = place()
            cots = jnp.concatenate([cot[...]] + [r[:, width:] for r in refs[:-2]], axis=0)
            for i, j in enumerate(js_now):
                for out, core in ((send, 1 - c), (keep, c)):
                    start = pl.multiple_of((offset + i) * 2 * blk + core * blk, LANES)
                    parts = [act[:, pl.ds(column(t ^ j, p, core), blk)]] + [r[:, pl.ds(start, blk)] for r in refs[:-2]]
                    out[i * blk : (i + 1) * blk, :] = contract(jnp.concatenate(parts, axis=0), cots, 0, 0)

        out = shape((len(js_now) * blk, vdim), f32)
        return kernel_call(body, [out, out], [activations, value_cotangent, *got], name="sums", cost=cost)

    def join(terms, pack, cost):
        def value(ref):
            return ref[...] if ref.shape[0] == blk else ref[:blk, :] * jnp.exp2(ref[blk : blk + 1, :])

        def body(*refs):
            out = refs[-1]
            total = sum((value(r) for r in refs[1:-1]), value(refs[0]))
            if not pack:
                out[...] = total
                return
            top = jnp.max(jnp.abs(total), axis=(0, 1), keepdims=True)
            power = jnp.clip(jnp.ceil(jnp.log(jnp.maximum(top, 1e-30)) * LOG2_E) - TOP_POWER, -110.0, 110.0)
            out[:blk, :] = total * jnp.exp2(-power)
            out[blk:, :] = jnp.broadcast_to(power, (PAD, vdim))

        (out,) = kernel_call(body, [shape((blk + PAD if pack else blk, vdim), f32)], terms, name="join", cost=cost)
        return out.astype(jnp.float16) if pack else out

    if OPT["sums_za"]:
        got[0], held[0] = barrier((got[0], held[0]))
    if OPT["sums_zb"]:
        got[0], *held = barrier((got[0], *held))
    if OPT["sums_qtr"]:
        got[0], acc = barrier((got[0], acc))
    if OPT["s_mode"] == "strip":
        firsts = [j for j in js if j.bit_count() > 1] or js[:1]
    else:
        firsts = js[: n_tensor // 2]
    others = [j for j in js if j not in firsts]
    keep_1, send_1 = sums_of(firsts, 0, OPT["c_sums1"])
    keep_2, send_2 = sums_of(others, len(firsts), OPT["c_sums2"])
    if OPT["ca_zb"]:
        send_1, held[-1] = barrier((send_1, held[-1]))
    mine = stack(held, OPT["c_mine"])
    if OPT["mine_after"]:
        mine, send_1 = barrier((mine, send_1))
    terms = {}
    for names, keep, twins_sum in ((firsts, keep_1, twin(send_1)), (others, keep_2, twin(send_2))):
        for i, j in enumerate(names):
            cut = slice(i * blk, (i + 1) * blk)
            terms[j] = [keep, twins_sum] if len(names) == 1 else [keep[cut], twins_sum[cut]]

    rows = (n_tensor - 1) * blk
    pieces = {0: [mine]}
    singles = [1 << b for b in range(chips.bit_length() - 1)]
    if OPT["w_mode"] == "pipe" and len(singles) > 1:
        cuts = [rows * i // len(singles) // 16 * 16 for i in range(len(singles))] + [rows]
    else:
        cuts = [0, rows]
    segs = [slice(a, b) for a, b in zip(cuts, cuts[1:])]
    for q in singles:
        pieces[q] = [across(mine[c] if len(segs) > 1 else mine, q) for c in segs]

    arrived = {}
    strip = OPT["s_mode"] == "strip"
    for j in js[:-1]:
        packed = join(terms[j], True, OPT["c_join1"] if j in firsts else OPT["c_join2"])
        if j == js[len(firsts)] and OPT["st2_after"]:
            _, *got_now = barrier((packed, *[x for q in singles for x in pieces[q]]))
            pieces.update({q: got_now[i * len(segs) : (i + 1) * len(segs)] for i, q in enumerate(singles)})
        arrived[j] = along(packed, j & -j if strip else j)
        if OPT["s1_after3"] and strip and j == js[len(firsts)]:
            for k in others[1:-1]:
                terms[k] = list(barrier((*terms[k], packed))[:-1])
        if strip and j in firsts:
            terms[j & (j - 1)].append(arrived[j].astype(f32))

    for q in sorted((q for q in range(1, chips) if q not in singles), key=lambda q: q.bit_count()):
        bits = [b for b in singles if q & b]
        if len(segs) > 1:
            pieces[q] = [across(pieces[q ^ bits[i % len(bits)]][i], bits[i % len(bits)]) for i in range(len(segs))]
            continue
        cuts = [rows * i // len(bits) // 16 * 16 for i in range(len(bits))] + [rows]
        ways = []
        for i, b in enumerate(bits):
            there = stack(pieces[q ^ b]) if len(pieces[q ^ b]) > 1 else pieces[q ^ b][0]
            ways.append(across(there[cuts[i] : cuts[i + 1]], b))
        pieces[q] = ways

    total = join(terms[0] + [arrived[j].astype(f32) for j in (others[:-1] if strip else js[:-1])], False, OPT["c_joinf"])
    weight_grad = total / jnp.sqrt(f32(tok * n_dp * n_tensor))
    if OPT["pf"]:
        acc, total = barrier((acc, total))

    def product(acc, grad, qs, last):
        n = (n_tensor - 1) * len(qs)
        ours = stack([x for q in qs for x in pieces[q]], OPT["c_e2stack"] if last else OPT["c_estack"])
        if last:
            after = [acc] * OPT["e2_acc"] + [arrived[1]] * OPT["e2_s1"] + [arrived[n_tensor // 2]] * OPT["e2_s2"]
            ours, *_ = barrier((ours, *after))
        elif OPT["e1_s"]:
            ours, *_ = barrier((ours, arrived[1]))
        operands = [ours, twin(ours)]

        def body(act, cot, acc, _, *refs):
            both, (out, grad, total, columns, sems) = refs[:2], refs[-5:]
            p, c, t = place()
            order = [(at_q * (n_tensor - 1) + i, q, j, core) for at_q, q in enumerate(qs) for i, j in enumerate(slots) for core in range(2)]
            weights = [both[k][at * blk : (at + 1) * blk, :] for at, _, _, k in order]
            columns_of = [pl.ds(column(t ^ j, p ^ q, (c, 1 - c)[k]), blk) for _, q, j, k in order]
            lhs = jnp.concatenate([act[:, cols] for cols in columns_of], axis=1)
            result = acc[...] + contract(lhs, jnp.concatenate(weights, axis=0), 1, 0)
            copies = []
            if last:
                total[...] = result.astype(bf16)
                copies.append(pltpu.make_async_copy(total, out, sems.at[n]))
                copies[0].start()
            else:
                out[...] = result
            for (at, q, j, k), w in zip(order, weights):
                cols = pl.ds(pl.multiple_of((c, 1 - c)[k] * blk, LANES), blk)
                columns[at, :, cols] = contract(cot[...], w, 1, 1).astype(bf16)
                if k:
                    copies.append(pltpu.make_async_copy(columns.at[at], grad.at[:, pl.ds(column(t ^ j, p ^ q), 2 * blk)], sems.at[at]))
                    copies[-1].start()
            for copy in copies:
                copy.wait()

        args = [activations, value_cotangent, acc, grad, *operands]
        return pl.pallas_call(
            body,
            out_shape=[shape((tok, vdim), bf16 if last else f32), shape((tok, depth), bf16)],
            in_specs=[whole] * 3 + [anywhere] + [whole] * len(operands),
            out_specs=[anywhere if last else whole, anywhere],
            scratch_shapes=[
                pltpu.VMEM((tok, vdim), bf16),
                pltpu.VMEM((n, tok, 2 * blk), bf16),
                pltpu.SemaphoreType.DMA((n + 1,)),
            ],
            input_output_aliases={3: 1},
            compiler_params=pltpu.CompilerParams(vmem_limit_bytes=VMEM_LIMIT),
            cost_estimate=pl.CostEstimate(flops=int((OPT["c_last"] if last else OPT["c_prod"]) * 1.15e9), bytes_accessed=1024, transcendentals=0),
            name="product",
        )(*args)

    late = [q for q in range(chips) if q.bit_count() >= 2]
    acc, grad = product(acc, grad, [0, *singles], not late)
    if late:
        acc, grad = product(acc, grad, late, True)
    return acc, grad, weight_grad


def solution(mesh):
    n_dp, n_tensor = mesh.shape["dp"], mesh.shape["tensor"]

    def per_device(activations, value_weight, value_cotangent):
        tok, depth = activations.shape
        powers = all(n > 1 and n & (n - 1) == 0 for n in (n_dp, n_tensor))
        if powers and depth % (n_dp * n_tensor * LANES) == 0 and tok % LANES == 0:
            return paired_form(n_dp, n_tensor, activations, value_weight, value_cotangent)
        return gathered_form(activations, value_weight, value_cotangent)

    return jax.shard_map(
        per_device,
        mesh=mesh,
        in_specs=(P(AXES, None), P("tensor", None), P(AXES, None)),
        out_specs=(P(AXES, None), P(AXES, None), P(("tensor", "dp"), None)),
        check_vma=False,
    )
```

```python
import functools

import jax
import jax.numpy as jnp
from jax import lax
from jax.experimental import pallas as pl
from jax.experimental.pallas import tpu as pltpu
from jax.sharding import PartitionSpec as P

OPT = {'pl': 0, 'jl': 0, 'ws2': 1, 'f1': 0, 'c_f1': 10, 'jk': 0, 'cot_first': 0, 'held_free': 1, 'c_cots': 10, 'slice_in': 'pack', 'st2_prod': 1, 's1_late': 0, 'c_joinl': 0, 'pf': 1, 's1_after3': 1, 'w_mode': 'whole', 'pack': 'vmem', 'pack_lim': 60, 's_mode': 'strip', 'z_mode': 'mix', 'e_mode': 'merged', 'sums_za': 0, 'sums_zb': 1, 'ca_zb': 0, 'mine_after': 0, 'st2_after': 0, 'e2_acc': 1, 'e2_s1': 1, 'e2_s2': 1, 'slice_after': 0, 'qtr_after': 'za', 'sums_qtr': 1, 'e1_s': 0, 'order': 'zs', 'c_pack': 0, 'c_slice': 0, 'c_zstack': 0, 'c_qtr': 0, 'c_sums1': 0, 'c_sums2': 0, 'c_join1': 0, 'c_join2': 0, 'c_joinf': 20, 'c_mine': 0, 'c_estack': 60, 'c_e2stack': 0, 'c_prod': 10, 'c_last': 0}
LANES = 128
PAD = 16
LOG2_E = 1.4426950408889634
TOP_POWER = 14.0
AXES = ("dp", "tensor")
VMEM_LIMIT = 32 * 1024 * 1024
PACK_LIMIT = 60 * 1024 * 1024


def contract(a, b, dim_a, dim_b):
    return lax.dot_general(a, b, (((dim_a,), (dim_b,)), ((), ())), preferred_element_type=jnp.float32)


def gathered_form(activations, value_weight, value_cotangent):
    tok_rows = activations.shape[0]
    full_weight = lax.all_gather(value_weight, "tensor", axis=0, tiled=True)
    value_proj = contract(activations, full_weight, 1, 0).astype(jnp.bfloat16)
    input_grad = contract(value_cotangent, full_weight, 1, 1).astype(jnp.bfloat16)
    own_columns = lax.all_to_all(activations, "tensor", split_axis=1, concat_axis=0, tiled=True)
    group_term = contract(own_columns, lax.all_gather(value_cotangent, "tensor", axis=0, tiled=True), 0, 0)
    summed = lax.psum_scatter(group_term, "dp", scatter_dimension=0, tiled=True)
    total_tokens = tok_rows * lax.axis_size("dp") * lax.axis_size("tensor")
    return value_proj, input_grad, summed / jnp.sqrt(jnp.float32(total_tokens))


def exchange(x, n_dp, n_tensor, dp_xor, tensor_xor):
    pairs = [(d * n_tensor + t, (d ^ dp_xor) * n_tensor + (t ^ tensor_xor)) for d in range(n_dp) for t in range(n_tensor)]
    return lax.ppermute(x, AXES, pairs)


def kernel_call(body, out_shapes, args, name, cost=0):
    whole = pl.BlockSpec(memory_space=pltpu.VMEM)
    return pl.pallas_call(
        body,
        out_shape=out_shapes,
        in_specs=[whole] * len(args),
        out_specs=[whole] * len(out_shapes),
        compiler_params=pltpu.CompilerParams(vmem_limit_bytes=VMEM_LIMIT),
        cost_estimate=pl.CostEstimate(flops=int(cost * 1.15e9), bytes_accessed=1024, transcendentals=0),
        name=name,
    )(*args)


def stack(parts, cost=0):
    parts = [p if isinstance(p, tuple) else (p, slice(0, p.shape[0])) for p in parts]

    def body(*refs):
        at = 0
        for ref, (_, cut) in zip(refs, parts):
            refs[-1][at : at + cut.stop - cut.start, :] = ref[cut, :]
            at += cut.stop - cut.start

    rows = sum(cut.stop - cut.start for _, cut in parts)
    out = jax.ShapeDtypeStruct((rows, parts[0][0].shape[1]), parts[0][0].dtype)
    return kernel_call(body, [out], [p for p, _ in parts], "stack", cost)[0]


def paired_form(n_dp, n_tensor, activations, value_weight, value_cotangent):
    tok, depth = activations.shape
    vdim = value_cotangent.shape[1]
    blk = depth // (n_dp * n_tensor)
    chips = n_dp // 2
    quarter = depth // n_tensor
    bf16, f32 = jnp.bfloat16, jnp.float32
    shape = jax.ShapeDtypeStruct
    barrier = lax.optimization_barrier

    def twin(x):
        return exchange(x, n_dp, n_tensor, 1, 0)

    def across(x, chip_xor):
        return exchange(x, n_dp, n_tensor, 2 * chip_xor, 0)

    def along(x, tensor_xor):
        return exchange(x, n_dp, n_tensor, 0, tensor_xor)

    def column(part, chip, core=0):
        return pl.multiple_of(((part * chips + chip) * 2 + core) * blk, LANES)

    def place():
        d = lax.axis_index("dp")
        return d // 2, d % 2, lax.axis_index("tensor")

    js = sorted(range(n_tensor), key=lambda j: (-j.bit_count(), -j)) if OPT["s_mode"] == "strip" else list(range(n_tensor - 1, -1, -1))
    width = n_tensor * 2 * blk

    if OPT["cot_first"]:
        cots = [across(value_cotangent, q) for q in range(1, chips)]
        all_cots = stack([value_cotangent, *cots], OPT["c_cots"])

    def pack_body(act, *outs):
        if not OPT["cot_first"]:
            cot, *outs = outs
        p, _, t = place()
        for q, out in enumerate(outs, 1):
            for i, j in enumerate(js):
                out[:, i * 2 * blk : (i + 1) * 2 * blk] = act[:, pl.ds(column(t ^ j, p ^ q), 2 * blk)]
            if not OPT["cot_first"]:
                out[:, width:] = cot[...]

    extra = 0 if OPT["cot_first"] else vdim

    def slice_body(weight, out):
        p, c, _ = place()
        out[...] = weight[pl.ds(pl.multiple_of((p * 2 + c) * blk, LANES), blk), :]

    if OPT["pack"] == "hbm":
        def pack_dma(act, cot, *refs):
            outs, sems = refs[:-1], refs[-1]
            p, _, t = place()
            pairs = []
            for q, out in enumerate(outs, 1):
                for i, j in enumerate(js):
                    pairs.append((act.at[:, pl.ds(column(t ^ j, p ^ q), 2 * blk)], out.at[:, i * 2 * blk : (i + 1) * 2 * blk]))
                pairs.append((cot, out.at[:, width:]))
            copies = [pltpu.make_async_copy(src, dst, sems.at[i]) for i, (src, dst) in enumerate(pairs)]
            for copy in copies:
                copy.start()
            for copy in copies:
                copy.wait()

        packs = pl.pallas_call(
            pack_dma,
            out_shape=[shape((tok, width + vdim), bf16)] * (chips - 1),
            in_specs=[pl.BlockSpec(memory_space=pltpu.HBM)] * 2,
            out_specs=[pl.BlockSpec(memory_space=pltpu.VMEM)] * (chips - 1),
            scratch_shapes=[pltpu.SemaphoreType.DMA(((chips - 1) * (n_tensor + 1),))],
            compiler_params=pltpu.CompilerParams(vmem_limit_bytes=int(OPT["pack_lim"] * 1024 * 1024)),
            cost_estimate=pl.CostEstimate(flops=int(OPT["c_pack"] * 1.15e9), bytes_accessed=1024, transcendentals=0),
            name="pack",
        )(activations, value_cotangent)
    else:
        packs = kernel_call(pack_body, [shape((tok, width + extra), bf16)] * (chips - 1), [activations] if OPT["cot_first"] else [activations, value_cotangent], name="pack", cost=OPT["c_pack"])
    sw = value_weight
    if OPT["slice_in"] == "cots":
        sw = barrier((value_weight, all_cots))[0]
    elif OPT["slice_in"] == "cot1":
        sw = barrier((value_weight, cots[0]))[0]
    elif OPT["slice_in"] == "pack":
        sw, *packs = barrier((value_weight, *packs))
    (own_slice,) = kernel_call(slice_body, [shape((blk, vdim), bf16)], [sw], name="own_slice", cost=OPT["c_slice"])
    if OPT["slice_after"]:
        own_slice, *packs = barrier((own_slice, *packs))
    got = [across(x, q) for q, x in enumerate(packs, 1)]

    if OPT["z_mode"] == "rec":
        held, slots = [own_slice], [0]
        bit = n_tensor // 2
        while bit:
            held.append(along(stack(held, OPT["c_zstack"]) if len(held) > 1 else held[0], bit))
            slots += [j ^ bit for j in slots]
            bit //= 2
        slots = slots[1:]
        held = held[1:]
    elif OPT["z_mode"] == "mix":
        slots = sorted(range(1, n_tensor), key=lambda j: (j.bit_count(), -j))
        by_slot = {0: own_slice}
        for j in slots:
            by_slot[j] = along(by_slot[j & (j - 1)], j & -j)
        held = [by_slot[j] for j in slots]
    else:
        slots = list(range(n_tensor - 1, 0, -1))
        held = [along(own_slice, j) for j in slots]

    def quarter_body(act, cot, w, acc, grad, columns, sem):
        _, _, t = place()
        own = pl.ds(pl.multiple_of(t * quarter, LANES), quarter)
        columns[...] = contract(cot[...], w[...], 1, 1).astype(bf16)
        copy = pltpu.make_async_copy(columns, grad.at[:, own], sem)
        copy.start()
        acc[...] = contract(act[:, own], w[...], 1, 0)
        copy.wait()

    whole, anywhere = pl.BlockSpec(memory_space=pltpu.VMEM), pl.BlockSpec(memory_space=pl.ANY)
    qw = value_weight
    if OPT["qtr_after"] == "pack":
        qw = barrier((value_weight, packs[0], got[0]))[0] if False else barrier((value_weight, own_slice))[0]
    elif OPT["qtr_after"] == "za":
        qw = barrier((value_weight, held[0]))[0]
    elif OPT["qtr_after"] == "a":
        qw = barrier((value_weight, got[0]))[0]
    acc, grad = pl.pallas_call(
        quarter_body,
        out_shape=[shape((tok, vdim), f32), shape((tok, depth), bf16)],
        in_specs=[whole] * 3,
        out_specs=[whole, anywhere],
        scratch_shapes=[pltpu.VMEM((tok, quarter), bf16), pltpu.SemaphoreType.DMA],
        compiler_params=pltpu.CompilerParams(vmem_limit_bytes=VMEM_LIMIT),
        cost_estimate=pl.CostEstimate(flops=int(OPT["c_qtr"] * 1.15e9), bytes_accessed=1024, transcendentals=0),
        name="own_quarter",
    )(activations, value_cotangent, value_weight)


    def sums_of(js_now, offset, cost):
        def body(act, cot, *refs):
            keep, send = refs[-2:]
            p, c, t = place()
            if OPT["cot_first"]:
                cots = cot[...]
            else:
                cots = jnp.concatenate([cot[...]] + [r[:, width:] for r in refs[:-2]], axis=0)
            for i, j in enumerate(js_now):
                for out, core in ((send, 1 - c), (keep, c)):
                    start = pl.multiple_of((offset + i) * 2 * blk + core * blk, LANES)
                    parts = [act[:, pl.ds(column(t ^ j, p, core), blk)]] + [r[:, pl.ds(start, blk)] for r in refs[:-2]]
                    out[i * blk : (i + 1) * blk, :] = contract(jnp.concatenate(parts, axis=0), cots, 0, 0)

        out = shape((len(js_now) * blk, vdim), f32)
        return kernel_call(body, [out, out], [activations, all_cots if OPT["cot_first"] else value_cotangent, *got], name="sums", cost=cost)

    def join(terms, pack, cost):
        def value(ref):
            return ref[...] if ref.shape[0] == blk else ref[:blk, :] * jnp.exp2(ref[blk : blk + 1, :])

        def body(*refs):
            out = refs[-1]
            total = sum((value(r) for r in refs[1:-1]), value(refs[0]))
            if not pack:
                out[...] = total
                return
            top = jnp.max(jnp.abs(total), axis=(0, 1), keepdims=True)
            power = jnp.clip(jnp.ceil(jnp.log(jnp.maximum(top, 1e-30)) * LOG2_E) - TOP_POWER, -110.0, 110.0)
            out[:blk, :] = total * jnp.exp2(-power)
            out[blk:, :] = jnp.broadcast_to(power, (PAD, vdim))

        (out,) = kernel_call(body, [shape((blk + PAD if pack else blk, vdim), f32)], terms, name="join", cost=cost)
        return out.astype(jnp.float16) if pack else out

    if OPT["sums_za"]:
        got[0], held[0] = barrier((got[0], held[0]))
    if OPT["sums_zb"] and OPT["held_free"]:
        got[0], *_ = barrier((got[0], *held))
    elif OPT["sums_zb"]:
        got[0], *held = barrier((got[0], *held))
    if OPT["sums_qtr"]:
        got[0], acc = barrier((got[0], acc))
    if OPT["s_mode"] == "strip":
        firsts = [j for j in js if j.bit_count() > 1] or js[:1]
    else:
        firsts = js[: n_tensor // 2]
    others = [j for j in js if j not in firsts]
    keep_1, send_1 = sums_of(firsts, 0, OPT["c_sums1"])
    keep_2, send_2 = sums_of(others, len(firsts), OPT["c_sums2"])
    if OPT["ca_zb"]:
        send_1, held[-1] = barrier((send_1, held[-1]))
    mine = stack(held, OPT["c_mine"])
    if OPT["mine_after"]:
        mine, send_1 = barrier((mine, send_1))
    if OPT["jk"]:
        keep_1, keep_2 = barrier((keep_1, keep_2))
    terms = {}
    for names, keep, twins_sum in ((firsts, keep_1, twin(send_1)), (others, keep_2, twin(send_2))):
        for i, j in enumerate(names):
            cut = slice(i * blk, (i + 1) * blk)
            terms[j] = [keep, twins_sum] if len(names) == 1 else [keep[cut], twins_sum[cut]]

    rows = (n_tensor - 1) * blk
    pieces = {0: [mine]}
    singles = [1 << b for b in range(chips.bit_length() - 1)]
    if OPT["w_mode"] == "pipe" and len(singles) > 1:
        cuts = [rows * i // len(singles) // 16 * 16 for i in range(len(singles))] + [rows]
    else:
        cuts = [0, rows]
    segs = [slice(a, b) for a, b in zip(cuts, cuts[1:])]
    for q in singles:
        pieces[q] = [across(mine[c] if len(segs) > 1 else mine, q) for c in segs]

    early = [q for q in range(chips) if q.bit_count() < 2]
    ours_early = stack([x for q in early for x in pieces[q]], OPT["c_estack"]) if OPT["ws2"] else None
    arrived = {}
    strip = OPT["s_mode"] == "strip"
    for j in js[:-1]:
        if OPT["ws2"] and j == js[len(firsts)]:
            terms[j][0], ours_early = barrier((terms[j][0], ours_early))
        packed = join(terms[j], True, OPT["c_join1"] if j in firsts else OPT["c_join2"])
        if j == js[len(firsts)] and OPT["st2_after"]:
            _, *got_now = barrier((packed, *[x for q in singles for x in pieces[q]]))
            pieces.update({q: got_now[i * len(segs) : (i + 1) * len(segs)] for i, q in enumerate(singles)})
        arrived[j] = along(packed, j & -j if strip else j)
        if OPT["f1"] and strip and j in firsts:
            nxt = j & (j - 1)
            mark = stack([(packed, slice(blk, blk + PAD))], OPT["c_f1"])
            terms[nxt][0] = barrier((terms[nxt][0], mark))[0]
        if OPT["s1_after3"] == 2 and strip and j == js[len(firsts)]:
            for k in others[1:-1]:
                terms[k] = list(barrier((*terms[k], *[pieces[q][0] for q in singles]))[: len(terms[k])])
        if OPT["s1_after3"] == 1 and strip and j == js[len(firsts)]:
            for k in others[1:-1]:
                terms[k] = list(barrier((*terms[k], packed))[:-1])
        if strip and j in firsts:
            terms[j & (j - 1)].append(arrived[j].astype(f32))

    for q in sorted((q for q in range(1, chips) if q not in singles), key=lambda q: q.bit_count()):
        bits = [b for b in singles if q & b]
        if len(segs) > 1:
            pieces[q] = [across(pieces[q ^ bits[i % len(bits)]][i], bits[i % len(bits)]) for i in range(len(segs))]
            continue
        cuts = [rows * i // len(bits) // 16 * 16 for i in range(len(bits))] + [rows]
        ways = []
        for i, b in enumerate(bits):
            there = stack(pieces[q ^ b]) if len(pieces[q ^ b]) > 1 else pieces[q ^ b][0]
            ways.append(across(there[cuts[i] : cuts[i + 1]], b))
        pieces[q] = ways

    def finish(after):
        own = terms[0]
        if after is not None:
            own = [*barrier((own[0], after))[:1], *own[1:]]
        if OPT["s1_late"]:
            total = join(own + [arrived[others[0]].astype(f32)], False, OPT["c_joinf"])
            return join([total] + [arrived[j].astype(f32) for j in others[1:-1]], False, OPT["c_joinl"])
        return join(own + [arrived[j].astype(f32) for j in (others[:-1] if strip else js[:-1])], False, OPT["c_joinf"])

    results = []
    if not OPT["jl"]:
        results.append(finish(None))
        if OPT["pf"]:
            acc, results[0] = barrier((acc, results[0]))

    def product(acc, grad, qs, last):
        n = (n_tensor - 1) * len(qs)
        if OPT["ws2"] and not last:
            ours = ours_early
        elif OPT["pl"] and last:
            ours = ours_late
        else:
            ours = stack([x for q in qs for x in pieces[q]], OPT["c_e2stack"] if last else OPT["c_estack"])
        if last:
            after = [acc] * OPT["e2_acc"] + [arrived[1]] * OPT["e2_s1"] + [arrived[n_tensor // 2]] * OPT["e2_s2"]
            if not OPT["pl"]:
                ours, *_ = barrier((ours, *after))
        elif OPT["e1_s"]:
            ours, *_ = barrier((ours, arrived[1]))
        operands = [ours, twin(ours)]
        if last and OPT["jl"]:
            results.append(finish(ours))

        def body(act, cot, acc, _, *refs):
            both, (out, grad, total, columns, sems) = refs[:2], refs[-5:]
            p, c, t = place()
            order = [(at_q * (n_tensor - 1) + i, q, j, core) for at_q, q in enumerate(qs) for i, j in enumerate(slots) for core in range(2)]
            weights = [both[k][at * blk : (at + 1) * blk, :] for at, _, _, k in order]
            columns_of = [pl.ds(column(t ^ j, p ^ q, (c, 1 - c)[k]), blk) for _, q, j, k in order]
            lhs = jnp.concatenate([act[:, cols] for cols in columns_of], axis=1)
            result = acc[...] + contract(lhs, jnp.concatenate(weights, axis=0), 1, 0)
            copies = []
            if last:
                total[...] = result.astype(bf16)
                copies.append(pltpu.make_async_copy(total, out, sems.at[n]))
                copies[0].start()
            else:
                out[...] = result
            for (at, q, j, k), w in zip(order, weights):
                cols = pl.ds(pl.multiple_of((c, 1 - c)[k] * blk, LANES), blk)
                columns[at, :, cols] = contract(cot[...], w, 1, 1).astype(bf16)
                if k:
                    copies.append(pltpu.make_async_copy(columns.at[at], grad.at[:, pl.ds(column(t ^ j, p ^ q), 2 * blk)], sems.at[at]))
                    copies[-1].start()
            for copy in copies:
                copy.wait()

        args = [activations, value_cotangent, acc, grad, *operands]
        return pl.pallas_call(
            body,
            out_shape=[shape((tok, vdim), bf16 if last else f32), shape((tok, depth), bf16)],
            in_specs=[whole] * 3 + [anywhere] + [whole] * len(operands),
            out_specs=[anywhere if last else whole, anywhere],
            scratch_shapes=[
                pltpu.VMEM((tok, vdim), bf16),
                pltpu.VMEM((n, tok, 2 * blk), bf16),
                pltpu.SemaphoreType.DMA((n + 1,)),
            ],
            input_output_aliases={3: 1},
            compiler_params=pltpu.CompilerParams(vmem_limit_bytes=VMEM_LIMIT),
            cost_estimate=pl.CostEstimate(flops=int((OPT["c_last"] if last else OPT["c_prod"]) * 1.15e9), bytes_accessed=1024, transcendentals=0),
            name="product",
        )(*args)

    late = [q for q in range(chips) if q.bit_count() >= 2]
    if OPT["pl"] and late:
        ours_late = stack([x for q in late for x in pieces[q]], OPT["c_e2stack"])
        acc, ours_late = barrier((acc, ours_late))
    acc, grad = product(acc, grad, [0, *singles], not late)
    if late:
        if OPT["st2_prod"]:
            acc, *parts = barrier((acc, *[x for q in late for x in pieces[q]]))
            for q in late:
                pieces[q], parts = parts[: len(pieces[q])], parts[len(pieces[q]) :]
        acc, grad = product(acc, grad, late, True)
    weight_grad = results[0] / jnp.sqrt(f32(tok * n_dp * n_tensor))
    return acc, grad, weight_grad


def solution(mesh):
    n_dp, n_tensor = mesh.shape["dp"], mesh.shape["tensor"]

    def per_device(activations, value_weight, value_cotangent):
        tok, depth = activations.shape
        powers = all(n > 1 and n & (n - 1) == 0 for n in (n_dp, n_tensor))
        if powers and depth % (n_dp * n_tensor * LANES) == 0 and tok % LANES == 0:
            return paired_form(n_dp, n_tensor, activations, value_weight, value_cotangent)
        return gathered_form(activations, value_weight, value_cotangent)

    return jax.shard_map(
        per_device,
        mesh=mesh,
        in_specs=(P(AXES, None), P("tensor", None), P(AXES, None)),
        out_specs=(P(AXES, None), P(AXES, None), P(("tensor", "dp"), None)),
        check_vma=False,
    )
```

```python
import math

import jax
import jax.numpy as jnp
from jax import lax
from jax.experimental import pallas as pl
from jax.experimental.pallas import tpu as pltpu
from jax.sharding import PartitionSpec as P

OPT = {'s1t': 0, 's1e': 0, 'tok': 1, 'jl': 0, 'c_pack': 0, 'c_slice': 0, 'c_qtr': 0, 'c_sums1': 30, 'c_sums2': 20, 'c_join1': 0, 'c_join2': 30, 'c_join3': 0, 'c_joinf': 5, 'c_mine': 0, 'c_estack': 60, 'c_e2stack': 0, 'c_prod': 0, 'c_last': 0, 's1p': 2, 'ws2': 1, 'st2_after': 2, 'e2p': 0, 'pt': 0}
LANES = 128
PAD = 16
LOG2_E = 1.4426950408889634
TOP_POWER = 14.0
AXES = ("dp", "tensor")
VMEM_LIMIT = 32 * 1024 * 1024
PACK_LIMIT = 60 * 1024 * 1024


def contract(a, b, dim_a, dim_b):
    return lax.dot_general(a, b, (((dim_a,), (dim_b,)), ((), ())), preferred_element_type=jnp.float32)


def gathered_form(activations, value_weight, value_cotangent):
    tok_rows = activations.shape[0]
    full_weight = lax.all_gather(value_weight, "tensor", axis=0, tiled=True)
    value_proj = contract(activations, full_weight, 1, 0).astype(jnp.bfloat16)
    input_grad = contract(value_cotangent, full_weight, 1, 1).astype(jnp.bfloat16)
    own_columns = lax.all_to_all(activations, "tensor", split_axis=1, concat_axis=0, tiled=True)
    group_term = contract(own_columns, lax.all_gather(value_cotangent, "tensor", axis=0, tiled=True), 0, 0)
    summed = lax.psum_scatter(group_term, "dp", scatter_dimension=0, tiled=True)
    total_tokens = tok_rows * lax.axis_size("dp") * lax.axis_size("tensor")
    return value_proj, input_grad, summed / jnp.sqrt(jnp.float32(total_tokens))


def exchange(x, n_dp, n_tensor, dp_xor, tensor_xor):
    pairs = [(d * n_tensor + t, (d ^ dp_xor) * n_tensor + (t ^ tensor_xor)) for d in range(n_dp) for t in range(n_tensor)]
    return lax.ppermute(x, AXES, pairs)


def estimate(cost):
    return pl.CostEstimate(flops=int(cost * 1.15e9), bytes_accessed=1024, transcendentals=0)


def kernel_call(body, out_shapes, args, name, cost=0):
    whole = pl.BlockSpec(memory_space=pltpu.VMEM)
    return pl.pallas_call(
        body,
        out_shape=out_shapes,
        in_specs=[whole] * len(args),
        out_specs=[whole] * len(out_shapes),
        compiler_params=pltpu.CompilerParams(vmem_limit_bytes=VMEM_LIMIT),
        cost_estimate=estimate(cost),
        name=name,
    )(*args)


def stack(parts, cost=0):
    parts = [p if isinstance(p, tuple) else (p, slice(0, p.shape[0])) for p in parts]

    def body(*refs):
        at = 0
        for ref, (_, cut) in zip(refs, parts):
            refs[-1][at : at + cut.stop - cut.start, :] = ref[cut, :]
            at += cut.stop - cut.start

    rows = sum(cut.stop - cut.start for _, cut in parts)
    out = jax.ShapeDtypeStruct((rows, parts[0][0].shape[1]), parts[0][0].dtype)
    return kernel_call(body, [out], [p for p, _ in parts], "stack", cost)[0]


def paired_form(n_dp, n_tensor, activations, value_weight, value_cotangent):
    tok, depth = activations.shape
    vdim = value_cotangent.shape[1]
    blk = depth // (n_dp * n_tensor)
    chips = n_dp // 2
    quarter = depth // n_tensor
    bf16, f32 = jnp.bfloat16, jnp.float32
    shape = jax.ShapeDtypeStruct
    barrier = lax.optimization_barrier
    whole, anywhere = pl.BlockSpec(memory_space=pltpu.VMEM), pl.BlockSpec(memory_space=pl.ANY)
    root = math.sqrt(tok * n_dp * n_tensor)

    def twin(x):
        return exchange(x, n_dp, n_tensor, 1, 0)

    def across(x, chip_xor):
        return exchange(x, n_dp, n_tensor, 2 * chip_xor, 0)

    def along(x, tensor_xor):
        return exchange(x, n_dp, n_tensor, 0, tensor_xor)

    def column(part, chip, core=0):
        return pl.multiple_of(((part * chips + chip) * 2 + core) * blk, LANES)

    def place():
        d = lax.axis_index("dp")
        return d // 2, d % 2, lax.axis_index("tensor")

    if OPT["s1e"]:
        js = sorted(range(1, n_tensor), key=lambda j: (-j.bit_count(), -j if j.bit_count() > 1 else j)) + [0]
    else:
        js = sorted(range(n_tensor), key=lambda j: (-j.bit_count(), -j))
    half = max(1, sum(j.bit_count() > 1 for j in js))
    width = n_tensor * 2 * blk

    def pack_body(act, cot, *outs):
        p, _, t = place()
        for q, out in enumerate(outs, 1):
            for i, j in enumerate(js):
                out[:, i * 2 * blk : (i + 1) * 2 * blk] = act[:, pl.ds(column(t ^ j, p ^ q), 2 * blk)]
            out[:, width:] = cot[...]

    def slice_body(weight, out):
        p, c, _ = place()
        out[...] = weight[pl.ds(pl.multiple_of((p * 2 + c) * blk, LANES), blk), :]

    packs = kernel_call(pack_body, [shape((tok, width + vdim), bf16)] * (chips - 1), [activations, value_cotangent], "pack", OPT["c_pack"])
    weight_then, *packs = barrier((value_weight, *packs))
    (own_slice,) = kernel_call(slice_body, [shape((blk, vdim), bf16)], [weight_then], "own_slice", OPT["c_slice"])
    got = [across(x, q) for q, x in enumerate(packs, 1)]

    slots = sorted(range(1, n_tensor), key=lambda j: (j.bit_count(), -j))
    by_slot = {0: own_slice}
    for j in slots:
        by_slot[j] = along(by_slot[j & (j - 1)], j & -j)
    held = [by_slot[j] for j in slots]

    def quarter_body(act, cot, w, acc, grad, columns, sem):
        _, _, t = place()
        own = pl.ds(pl.multiple_of(t * quarter, LANES), quarter)
        columns[...] = contract(cot[...], w[...], 1, 1).astype(bf16)
        copy = pltpu.make_async_copy(columns, grad.at[:, own], sem)
        copy.start()
        acc[...] = contract(act[:, own], w[...], 1, 0)
        copy.wait()

    weight_then, _ = barrier((value_weight, held[0]))
    acc, grad = pl.pallas_call(
        quarter_body,
        out_shape=[shape((tok, vdim), f32), shape((tok, depth), bf16)],
        in_specs=[whole] * 3,
        out_specs=[whole, anywhere],
        scratch_shapes=[pltpu.VMEM((tok, quarter), bf16), pltpu.SemaphoreType.DMA],
        compiler_params=pltpu.CompilerParams(vmem_limit_bytes=VMEM_LIMIT),
        cost_estimate=estimate(OPT["c_qtr"]),
        name="own_quarter",
    )(activations, value_cotangent, weight_then)

    def sums_of(js_now, offset, cost):
        def body(act, cot, *refs):
            keep, send = refs[-2:]
            p, c, t = place()
            cots = jnp.concatenate([cot[...]] + [r[:, width:] for r in refs[:-2]], axis=0)
            for i, j in enumerate(js_now):
                for out, core in ((send, 1 - c), (keep, c)):
                    start = pl.multiple_of((offset + i) * 2 * blk + core * blk, LANES)
                    parts = [act[:, pl.ds(column(t ^ j, p, core), blk)]] + [r[:, pl.ds(start, blk)] for r in refs[:-2]]
                    out[i * blk : (i + 1) * blk, :] = contract(jnp.concatenate(parts, axis=0), cots, 0, 0)

        out = shape((len(js_now) * blk, vdim), f32)
        return kernel_call(body, [out, out], [activations, value_cotangent, *got], "sums", cost)

    def join(groups, pack, cost, after=()):
        arrays = []
        for group in groups:
            arrays += [a for a, _, _ in group if not any(a is b for b in arrays)]
        found = [[([a is b for b in arrays].index(True), at, power_at) for a, at, power_at in g] for g in groups]
        rows = len(groups) * blk

        def body(*refs):
            out = refs[-1]

            def value(k, at, power_at):
                x = refs[k][at : at + blk, :]
                return x if power_at is None else x * jnp.exp2(refs[k][power_at : power_at + 1, :])

            totals = []
            for g in found:
                total = value(*g[0])
                for term in g[1:]:
                    total = total + value(*term)
                totals.append(total)
            total = jnp.concatenate(totals, axis=0)
            if not pack:
                out[...] = total
                return
            top = jnp.max(jnp.abs(total), axis=(0, 1), keepdims=True)
            power = jnp.clip(jnp.ceil(jnp.log(jnp.maximum(top, 1e-30)) * LOG2_E) - TOP_POWER, -110.0, 110.0)
            out[:rows, :] = total * jnp.exp2(-power)
            out[rows:, :] = jnp.broadcast_to(power, (PAD, vdim))

        (out,) = kernel_call(body, [shape((rows + PAD if pack else rows, vdim), f32)], [*arrays, *after], "join", cost)
        return out.astype(jnp.float16) if pack else out

    got[0], acc, *_ = barrier((got[0], acc, *held))
    keep_1, send_1 = sums_of(js[:half], 0, OPT["c_sums1"])
    keep_2, send_2 = sums_of(js[half:], half, OPT["c_sums2"])
    mine = stack(held, OPT["c_mine"])
    twin_1, twin_2 = twin(send_1), twin(send_2)
    terms = {j: [(keep_1, i * blk, None), (twin_1, i * blk, None)] for i, j in enumerate(js[:half])}
    terms.update({j: [(keep_2, i * blk, None), (twin_2, i * blk, None)] for i, j in enumerate(js[half:])})

    rows = (n_tensor - 1) * blk
    singles = [1 << b for b in range(chips.bit_length() - 1)]
    late = [q for q in range(chips) if q.bit_count() >= 2]
    pieces = {0: [mine], **{q: [across(mine, q)] for q in singles}}

    def product(acc, grad, qs, ours, total=None, twins=None):
        last = total is not None
        n = (n_tensor - 1) * len(qs)

        def body(act, cot, acc, _, mine, twins, *refs):
            both = mine, twins
            p, c, t = place()
            if last:
                total, proj, grad, weight_grad, proj_out, grad_out, columns, sems = refs
                grad_out[...] = total[...] * (1.0 / root)
                copies = [pltpu.make_async_copy(grad_out, weight_grad, sems.at[n + 1])]
                copies[0].start()
            else:
                out, grad, columns, sems = refs
                copies = []
            order = [(at_q * (n_tensor - 1) + i, q, j, core) for at_q, q in enumerate(qs) for i, j in enumerate(slots) for core in range(2)]
            weights = [both[k][at * blk : (at + 1) * blk, :] for at, _, _, k in order]
            columns_of = [pl.ds(column(t ^ j, p ^ q, (c, 1 - c)[k]), blk) for _, q, j, k in order]
            lhs = jnp.concatenate([act[:, cols] for cols in columns_of], axis=1)
            result = acc[...] + contract(lhs, jnp.concatenate(weights, axis=0), 1, 0)
            if last:
                proj_out[...] = result.astype(bf16)
                copies.append(pltpu.make_async_copy(proj_out, proj, sems.at[n]))
                copies[-1].start()
            else:
                out[...] = result
            for (at, q, j, k), w in zip(order, weights):
                cols = pl.ds(pl.multiple_of((c, 1 - c)[k] * blk, LANES), blk)
                columns[at, :, cols] = contract(cot[...], w, 1, 1).astype(bf16)
                if k:
                    copies.append(pltpu.make_async_copy(columns.at[at], grad.at[:, pl.ds(column(t ^ j, p ^ q), 2 * blk)], sems.at[at]))
                    copies[-1].start()
            for copy in copies:
                copy.wait()

        args = [activations, value_cotangent, acc, grad, ours, twin(ours) if twins is None else twins] + [total] * last
        outs = [shape((tok, vdim), bf16 if last else f32), shape((tok, depth), bf16)] + [shape((blk, vdim), f32)] * last
        scratch = [pltpu.VMEM((tok, vdim), bf16), pltpu.VMEM((blk, vdim), f32)] * last
        return pl.pallas_call(
            body,
            out_shape=outs,
            in_specs=[whole] * 3 + [anywhere] + [whole] * (2 + last),
            out_specs=[anywhere] * 3 if last else [whole, anywhere],
            scratch_shapes=scratch + [pltpu.VMEM((n, tok, 2 * blk), bf16), pltpu.SemaphoreType.DMA((n + 2,))],
            input_output_aliases={3: 1},
            compiler_params=pltpu.CompilerParams(vmem_limit_bytes=VMEM_LIMIT),
            cost_estimate=estimate(OPT["c_last"] if last else OPT["c_prod"]),
            name="product",
        )(*args)

    def tie(j, x):
        (a, at, power_at), *others = terms[j]
        a, x = barrier((a, x))
        terms[j] = [(a, at, power_at), *others]
        return x

    early, ours_early, done = [0, *singles], None, False
    for i, j in enumerate(js[:-1]):
        last_hop = i == (n_tensor - 2 if OPT["s1e"] else half)
        if last_hop:
            if OPT["s1e"] and i > half:
                arrived = tie(j, arrived)
                (x, at, power_at) = terms[0][-1]
                terms[0][-1] = (arrived, at, power_at)
            ours_early = stack([x for q in early for x in pieces[q]], OPT["c_estack"])
            if OPT["ws2"]:
                ours_early = tie(j, ours_early)
        if i == half and OPT["s1p"] == 2:
            twin_early = twin(ours_early)
        if not OPT["s1e"] and i > half and OPT["s1p"] == 2:
            twin_early = tie(j, twin_early)
        if not OPT["s1e"] and i > half and not done and late and OPT["s1p"] < 2:
            acc, grad = product(acc, grad, early, ours_early)
            done = True
        if i > half and done and OPT["s1p"] == 1:
            acc = tie(j, acc)
        packed = join([terms[j]], True, OPT["c_join1"] if i < half else OPT["c_join2"] if last_hop else OPT["c_join3"])
        if i == half - 1 and OPT["s1t"] and len(js) > half + 2:
            packed = tie(js[half], packed)
        if i == (half if OPT["s1e"] and len(js) > half + 2 else 0) and OPT["st2_after"] == 2:
            _, *then = barrier((packed, *[pieces[q][0] for q in singles]))
            pieces.update({q: [x] for q, x in zip(singles, then)})
        arrived = along(packed, j & -j).astype(f32)
        terms[j & (j - 1)].append((arrived, 0, blk))
    if ours_early is None:
        ours_early = stack([x for q in early for x in pieces[q]], OPT["c_estack"])
    if late and not done:
        acc, grad = product(acc, grad, early, ours_early, None, twin_early if OPT["s1p"] == 2 else None)

    if late and OPT["pt"]:
        acc = tie(0, acc)
    after = [twin(acc[:8, :LANES])] if OPT["tok"] and late else []
    if not OPT["jl"] or not late:
        total = join([terms[0]], False, OPT["c_joinf"], after)
    if not late:
        return product(acc, grad, early, ours_early, total)
    for q in sorted(late, key=lambda q: q.bit_count()):
        bits = [b for b in singles if q & b]
        cuts = [rows * i // len(bits) // 16 * 16 for i in range(len(bits))] + [rows]
        ways = []
        for i, b in enumerate(bits):
            there = stack(pieces[q ^ b]) if len(pieces[q ^ b]) > 1 else pieces[q ^ b][0]
            ways.append(across(there[cuts[i] : cuts[i + 1]], b))
        pieces[q] = ways
    ours_late = stack([x for q in late for x in pieces[q]], OPT["c_e2stack"])
    if OPT["jl"]:
        ours_late = tie(0, ours_late)
        total = join([terms[0]], False, OPT["c_joinf"])
    if OPT["e2p"]:
        ours_late, acc = barrier((ours_late, acc))
    return product(acc, grad, late, ours_late, total)


def solution(mesh):
    n_dp, n_tensor = mesh.shape["dp"], mesh.shape["tensor"]

    def per_device(activations, value_weight, value_cotangent):
        tok, depth = activations.shape
        powers = all(n > 1 and n & (n - 1) == 0 for n in (n_dp, n_tensor))
        if powers and depth % (n_dp * n_tensor * LANES) == 0 and tok % LANES == 0:
            return paired_form(n_dp, n_tensor, activations, value_weight, value_cotangent)
        return gathered_form(activations, value_weight, value_cotangent)

    return jax.shard_map(
        per_device,
        mesh=mesh,
        in_specs=(P(AXES, None), P("tensor", None), P(AXES, None)),
        out_specs=(P(AXES, None), P(AXES, None), P(("tensor", "dp"), None)),
        check_vma=False,
    )
```

```python
import math

import jax
import jax.numpy as jnp
from jax import lax
from jax.experimental import pallas as pl
from jax.experimental.pallas import tpu as pltpu
from jax.sharding import PartitionSpec as P

LANES = 128
PAD = 16
LOG2_E = 1.4426950408889634
TOP_POWER = 14.0
AXES = ("dp", "tensor")
VMEM_LIMIT = 32 * 1024 * 1024


def contract(a, b, dim_a, dim_b):
    return lax.dot_general(a, b, (((dim_a,), (dim_b,)), ((), ())), preferred_element_type=jnp.float32)


def gathered_form(activations, value_weight, value_cotangent):
    tok_rows = activations.shape[0]
    full_weight = lax.all_gather(value_weight, "tensor", axis=0, tiled=True)
    value_proj = contract(activations, full_weight, 1, 0).astype(jnp.bfloat16)
    input_grad = contract(value_cotangent, full_weight, 1, 1).astype(jnp.bfloat16)
    own_columns = lax.all_to_all(activations, "tensor", split_axis=1, concat_axis=0, tiled=True)
    group_term = contract(own_columns, lax.all_gather(value_cotangent, "tensor", axis=0, tiled=True), 0, 0)
    summed = lax.psum_scatter(group_term, "dp", scatter_dimension=0, tiled=True)
    total_tokens = tok_rows * lax.axis_size("dp") * lax.axis_size("tensor")
    return value_proj, input_grad, summed / jnp.sqrt(jnp.float32(total_tokens))


def exchange(x, n_dp, n_tensor, dp_xor, tensor_xor):
    pairs = [(d * n_tensor + t, (d ^ dp_xor) * n_tensor + (t ^ tensor_xor)) for d in range(n_dp) for t in range(n_tensor)]
    return lax.ppermute(x, AXES, pairs)


def estimate(cost):
    return pl.CostEstimate(flops=int(cost * 1.15e9), bytes_accessed=1024, transcendentals=0)


def kernel_call(body, out_shapes, args, name, cost=0):
    whole = pl.BlockSpec(memory_space=pltpu.VMEM)
    return pl.pallas_call(
        body,
        out_shape=out_shapes,
        in_specs=[whole] * len(args),
        out_specs=[whole] * len(out_shapes),
        compiler_params=pltpu.CompilerParams(vmem_limit_bytes=VMEM_LIMIT),
        cost_estimate=estimate(cost),
        name=name,
    )(*args)


def stack(parts, cost=0):
    parts = [p if isinstance(p, tuple) else (p, slice(0, p.shape[0])) for p in parts]

    def body(*refs):
        at = 0
        for ref, (_, cut) in zip(refs, parts):
            refs[-1][at : at + cut.stop - cut.start, :] = ref[cut, :]
            at += cut.stop - cut.start

    rows = sum(cut.stop - cut.start for _, cut in parts)
    out = jax.ShapeDtypeStruct((rows, parts[0][0].shape[1]), parts[0][0].dtype)
    return kernel_call(body, [out], [p for p, _ in parts], "stack", cost)[0]


def paired_form(n_dp, n_tensor, activations, value_weight, value_cotangent):
    tok, depth = activations.shape
    vdim = value_cotangent.shape[1]
    blk = depth // (n_dp * n_tensor)
    chips = n_dp // 2
    quarter = depth // n_tensor
    bf16, f32 = jnp.bfloat16, jnp.float32
    shape = jax.ShapeDtypeStruct
    barrier = lax.optimization_barrier
    whole, anywhere = pl.BlockSpec(memory_space=pltpu.VMEM), pl.BlockSpec(memory_space=pl.ANY)
    root = math.sqrt(tok * n_dp * n_tensor)

    def twin(x):
        return exchange(x, n_dp, n_tensor, 1, 0)

    def across(x, chip_xor):
        return exchange(x, n_dp, n_tensor, 2 * chip_xor, 0)

    def along(x, tensor_xor):
        return exchange(x, n_dp, n_tensor, 0, tensor_xor)

    def column(part, chip, core=0):
        return pl.multiple_of(((part * chips + chip) * 2 + core) * blk, LANES)

    def place():
        d = lax.axis_index("dp")
        return d // 2, d % 2, lax.axis_index("tensor")

    js = sorted(range(n_tensor), key=lambda j: (-j.bit_count(), -j))
    half = max(1, sum(j.bit_count() > 1 for j in js))
    width = n_tensor * 2 * blk

    def pack_body(act, cot, *outs):
        p, _, t = place()
        for q, out in enumerate(outs, 1):
            for i, j in enumerate(js):
                out[:, i * 2 * blk : (i + 1) * 2 * blk] = act[:, pl.ds(column(t ^ j, p ^ q), 2 * blk)]
            out[:, width:] = cot[...]

    def slice_body(weight, out):
        p, c, _ = place()
        out[...] = weight[pl.ds(pl.multiple_of((p * 2 + c) * blk, LANES), blk), :]

    packs = kernel_call(pack_body, [shape((tok, width + vdim), bf16)] * (chips - 1), [activations, value_cotangent], "pack")
    weight_then, *packs = barrier((value_weight, *packs))
    (own_slice,) = kernel_call(slice_body, [shape((blk, vdim), bf16)], [weight_then], "own_slice")
    got = [across(x, q) for q, x in enumerate(packs, 1)]

    slots = sorted(range(1, n_tensor), key=lambda j: (j.bit_count(), -j))
    by_slot = {0: own_slice}
    for j in slots:
        by_slot[j] = along(by_slot[j & (j - 1)], j & -j)
    held = [by_slot[j] for j in slots]

    def quarter_body(act, cot, w, acc, grad, columns, sem):
        _, _, t = place()
        own = pl.ds(pl.multiple_of(t * quarter, LANES), quarter)
        columns[...] = contract(cot[...], w[...], 1, 1).astype(bf16)
        copy = pltpu.make_async_copy(columns, grad.at[:, own], sem)
        copy.start()
        acc[...] = contract(act[:, own], w[...], 1, 0)
        copy.wait()

    weight_then, _ = barrier((value_weight, held[0]))
    acc, grad = pl.pallas_call(
        quarter_body,
        out_shape=[shape((tok, vdim), f32), shape((tok, depth), bf16)],
        in_specs=[whole] * 3,
        out_specs=[whole, anywhere],
        scratch_shapes=[pltpu.VMEM((tok, quarter), bf16), pltpu.SemaphoreType.DMA],
        compiler_params=pltpu.CompilerParams(vmem_limit_bytes=VMEM_LIMIT),
        cost_estimate=estimate(0),
        name="own_quarter",
    )(activations, value_cotangent, weight_then)

    def sums_of(js_now, offset, cost):
        def body(act, cot, *refs):
            keep, send = refs[-2:]
            p, c, t = place()
            cots = jnp.concatenate([cot[...]] + [r[:, width:] for r in refs[:-2]], axis=0)
            for i, j in enumerate(js_now):
                for out, core in ((send, 1 - c), (keep, c)):
                    start = pl.multiple_of((offset + i) * 2 * blk + core * blk, LANES)
                    parts = [act[:, pl.ds(column(t ^ j, p, core), blk)]] + [r[:, pl.ds(start, blk)] for r in refs[:-2]]
                    out[i * blk : (i + 1) * blk, :] = contract(jnp.concatenate(parts, axis=0), cots, 0, 0)

        out = shape((len(js_now) * blk, vdim), f32)
        return kernel_call(body, [out, out], [activations, value_cotangent, *got], "sums", cost)

    def join(groups, pack, cost, after=()):
        arrays = []
        for group in groups:
            arrays += [a for a, _, _ in group if not any(a is b for b in arrays)]
        found = [[([a is b for b in arrays].index(True), at, power_at) for a, at, power_at in g] for g in groups]
        rows = len(groups) * blk

        def body(*refs):
            out = refs[-1]

            def value(k, at, power_at):
                x = refs[k][at : at + blk, :]
                return x if power_at is None else x * jnp.exp2(refs[k][power_at : power_at + 1, :])

            totals = []
            for g in found:
                total = value(*g[0])
                for term in g[1:]:
                    total = total + value(*term)
                totals.append(total)
            total = jnp.concatenate(totals, axis=0)
            if not pack:
                out[...] = total
                return
            top = jnp.max(jnp.abs(total), axis=(0, 1), keepdims=True)
            power = jnp.clip(jnp.ceil(jnp.log(jnp.maximum(top, 1e-30)) * LOG2_E) - TOP_POWER, -110.0, 110.0)
            out[:rows, :] = total * jnp.exp2(-power)
            out[rows:, :] = jnp.broadcast_to(power, (PAD, vdim))

        (out,) = kernel_call(body, [shape((rows + PAD if pack else rows, vdim), f32)], [*arrays, *after], "join", cost)
        return out.astype(jnp.float16) if pack else out

    got[0], acc, *_ = barrier((got[0], acc, *held))
    keep_1, send_1 = sums_of(js[:half], 0, 30)
    keep_2, send_2 = sums_of(js[half:], half, 20)
    mine = stack(held)
    twin_1, twin_2 = twin(send_1), twin(send_2)
    terms = {j: [(keep_1, i * blk, None), (twin_1, i * blk, None)] for i, j in enumerate(js[:half])}
    terms.update({j: [(keep_2, i * blk, None), (twin_2, i * blk, None)] for i, j in enumerate(js[half:])})

    rows = (n_tensor - 1) * blk
    singles = [1 << b for b in range(chips.bit_length() - 1)]
    late = [q for q in range(chips) if q.bit_count() >= 2]
    pieces = {0: [mine], **{q: [across(mine, q)] for q in singles}}

    def product(acc, grad, qs, ours, twins, total=None):
        last = total is not None
        n = (n_tensor - 1) * len(qs)

        def body(act, cot, acc, _, mine, twins, *refs):
            both = mine, twins
            p, c, t = place()
            if last:
                total, proj, grad, weight_grad, proj_out, grad_out, columns, sems = refs
                grad_out[...] = total[...] * (1.0 / root)
                copies = [pltpu.make_async_copy(grad_out, weight_grad, sems.at[n + 1])]
                copies[0].start()
            else:
                out, grad, columns, sems = refs
                copies = []
            order = [(at_q * (n_tensor - 1) + i, q, j, core) for at_q, q in enumerate(qs) for i, j in enumerate(slots) for core in range(2)]
            weights = [both[k][at * blk : (at + 1) * blk, :] for at, _, _, k in order]
            columns_of = [pl.ds(column(t ^ j, p ^ q, (c, 1 - c)[k]), blk) for _, q, j, k in order]
            lhs = jnp.concatenate([act[:, cols] for cols in columns_of], axis=1)
            result = acc[...] + contract(lhs, jnp.concatenate(weights, axis=0), 1, 0)
            if last:
                proj_out[...] = result.astype(bf16)
                copies.append(pltpu.make_async_copy(proj_out, proj, sems.at[n]))
                copies[-1].start()
            else:
                out[...] = result
            for (at, q, j, k), w in zip(order, weights):
                cols = pl.ds(pl.multiple_of((c, 1 - c)[k] * blk, LANES), blk)
                columns[at, :, cols] = contract(cot[...], w, 1, 1).astype(bf16)
                if k:
                    copies.append(pltpu.make_async_copy(columns.at[at], grad.at[:, pl.ds(column(t ^ j, p ^ q), 2 * blk)], sems.at[at]))
                    copies[-1].start()
            for copy in copies:
                copy.wait()

        args = [activations, value_cotangent, acc, grad, ours, twins] + [total] * last
        outs = [shape((tok, vdim), bf16 if last else f32), shape((tok, depth), bf16)] + [shape((blk, vdim), f32)] * last
        scratch = [pltpu.VMEM((tok, vdim), bf16), pltpu.VMEM((blk, vdim), f32)] * last
        return pl.pallas_call(
            body,
            out_shape=outs,
            in_specs=[whole] * 3 + [anywhere] + [whole] * (2 + last),
            out_specs=[anywhere] * 3 if last else [whole, anywhere],
            scratch_shapes=scratch + [pltpu.VMEM((n, tok, 2 * blk), bf16), pltpu.SemaphoreType.DMA((n + 2,))],
            input_output_aliases={3: 1},
            compiler_params=pltpu.CompilerParams(vmem_limit_bytes=VMEM_LIMIT),
            cost_estimate=estimate(0),
            name="product",
        )(*args)

    def tie(j, x):
        (a, at, power_at), *others = terms[j]
        a, x = barrier((a, x))
        terms[j] = [(a, at, power_at), *others]
        return x

    early, ours_early = [0, *singles], None
    for i, j in enumerate(js[:-1]):
        if i == half:
            ours_early = tie(j, stack([x for q in early for x in pieces[q]], 60))
            twin_early = twin(ours_early)
        if i > half:
            twin_early = tie(j, twin_early)
        packed = join([terms[j]], True, 30 if i == half else 0)
        if i == 0:
            _, *then = barrier((packed, *[pieces[q][0] for q in singles]))
            pieces.update({q: [x] for q, x in zip(singles, then)})
        arrived = along(packed, j & -j).astype(f32)
        terms[j & (j - 1)].append((arrived, 0, blk))
    if ours_early is None:
        ours_early = stack([x for q in early for x in pieces[q]], 60)
        twin_early = twin(ours_early)
    if not late:
        return product(acc, grad, early, ours_early, twin_early, join([terms[0]], False, 5))
    acc, grad = product(acc, grad, early, ours_early, twin_early)

    total = join([terms[0]], False, 5, [twin(acc[:8, :LANES])])
    for q in sorted(late, key=lambda q: q.bit_count()):
        bits = [b for b in singles if q & b]
        cuts = [rows * i // len(bits) // 16 * 16 for i in range(len(bits))] + [rows]
        ways = []
        for i, b in enumerate(bits):
            there = stack(pieces[q ^ b]) if len(pieces[q ^ b]) > 1 else pieces[q ^ b][0]
            ways.append(across(there[cuts[i] : cuts[i + 1]], b))
        pieces[q] = ways
    ours_late = stack([x for q in late for x in pieces[q]])
    return product(acc, grad, late, ours_late, twin(ours_late), total)


def solution(mesh):
    n_dp, n_tensor = mesh.shape["dp"], mesh.shape["tensor"]

    def per_device(activations, value_weight, value_cotangent):
        tok, depth = activations.shape
        powers = all(n > 1 and n & (n - 1) == 0 for n in (n_dp, n_tensor))
        if powers and depth % (n_dp * n_tensor * LANES) == 0 and tok % LANES == 0:
            return paired_form(n_dp, n_tensor, activations, value_weight, value_cotangent)
        return gathered_form(activations, value_weight, value_cotangent)

    return jax.shard_map(
        per_device,
        mesh=mesh,
        in_specs=(P(AXES, None), P("tensor", None), P(AXES, None)),
        out_specs=(P(AXES, None), P(AXES, None), P(("tensor", "dp"), None)),
        check_vma=False,
    )
```

```python
import math

import jax
import jax.numpy as jnp
from jax import lax
from jax.experimental import pallas as pl
from jax.experimental.pallas import tpu as pltpu
from jax.sharding import PartitionSpec as P

LANES = 128
PAD = 16
LOG2_E = 1.4426950408889634
TOP_POWER = 14.0
AXES = ("dp", "tensor")
VMEM_LIMIT = 32 * 1024 * 1024


def contract(a, b, dim_a, dim_b):
    return lax.dot_general(a, b, (((dim_a,), (dim_b,)), ((), ())), preferred_element_type=jnp.float32)


def gathered_form(activations, value_weight, value_cotangent):
    tok_rows = activations.shape[0]
    full_weight = lax.all_gather(value_weight, "tensor", axis=0, tiled=True)
    value_proj = contract(activations, full_weight, 1, 0).astype(jnp.bfloat16)
    input_grad = contract(value_cotangent, full_weight, 1, 1).astype(jnp.bfloat16)
    own_columns = lax.all_to_all(activations, "tensor", split_axis=1, concat_axis=0, tiled=True)
    group_term = contract(own_columns, lax.all_gather(value_cotangent, "tensor", axis=0, tiled=True), 0, 0)
    summed = lax.psum_scatter(group_term, "dp", scatter_dimension=0, tiled=True)
    total_tokens = tok_rows * lax.axis_size("dp") * lax.axis_size("tensor")
    return value_proj, input_grad, summed / jnp.sqrt(jnp.float32(total_tokens))


def exchange(x, n_dp, n_tensor, dp_xor, tensor_xor):
    pairs = [(d * n_tensor + t, (d ^ dp_xor) * n_tensor + (t ^ tensor_xor)) for d in range(n_dp) for t in range(n_tensor)]
    return lax.ppermute(x, AXES, pairs)


def estimate(cost):
    return pl.CostEstimate(flops=int(cost * 1.15e9), bytes_accessed=1024, transcendentals=0)


def kernel_call(body, out_shapes, args, name, cost=0):
    whole = pl.BlockSpec(memory_space=pltpu.VMEM)
    return pl.pallas_call(
        body,
        out_shape=out_shapes,
        in_specs=[whole] * len(args),
        out_specs=[whole] * len(out_shapes),
        compiler_params=pltpu.CompilerParams(vmem_limit_bytes=VMEM_LIMIT),
        cost_estimate=estimate(cost),
        name=name,
    )(*args)


def stack(parts, cost=0):
    parts = [p if isinstance(p, tuple) else (p, slice(0, p.shape[0])) for p in parts]

    def body(*refs):
        at = 0
        for ref, (_, cut) in zip(refs, parts):
            refs[-1][at : at + cut.stop - cut.start, :] = ref[cut, :]
            at += cut.stop - cut.start

    rows = sum(cut.stop - cut.start for _, cut in parts)
    out = jax.ShapeDtypeStruct((rows, parts[0][0].shape[1]), parts[0][0].dtype)
    return kernel_call(body, [out], [p for p, _ in parts], "stack", cost)[0]


def paired_form(n_dp, n_tensor, activations, value_weight, value_cotangent):
    tok, depth = activations.shape
    vdim = value_cotangent.shape[1]
    blk = depth // (n_dp * n_tensor)
    chips = n_dp // 2
    quarter = depth // n_tensor
    bf16, f32 = jnp.bfloat16, jnp.float32
    shape = jax.ShapeDtypeStruct
    barrier = lax.optimization_barrier
    whole, anywhere = pl.BlockSpec(memory_space=pltpu.VMEM), pl.BlockSpec(memory_space=pl.ANY)
    root = math.sqrt(tok * n_dp * n_tensor)

    def twin(x):
        return exchange(x, n_dp, n_tensor, 1, 0)

    def across(x, chip_xor):
        return exchange(x, n_dp, n_tensor, 2 * chip_xor, 0)

    def along(x, tensor_xor):
        return exchange(x, n_dp, n_tensor, 0, tensor_xor)

    def column(part, chip, core=0):
        return pl.multiple_of(((part * chips + chip) * 2 + core) * blk, LANES)

    def place():
        d = lax.axis_index("dp")
        return d // 2, d % 2, lax.axis_index("tensor")

    js = sorted(range(n_tensor), key=lambda j: (-j.bit_count(), -j))
    half = max(1, sum(j.bit_count() > 1 for j in js))
    width = n_tensor * 2 * blk

    both = jnp.concatenate([activations, value_cotangent], axis=1)

    def pack_body(both, *outs):
        p, _, t = place()
        for q, out in enumerate(outs, 1):
            for i, j in enumerate(js):
                out[:, i * 2 * blk : (i + 1) * 2 * blk] = both[:, pl.ds(column(t ^ j, p ^ q), 2 * blk)]
            out[:, width:] = both[:, depth:]

    def slice_body(weight, out):
        p, c, _ = place()
        out[...] = weight[pl.ds(pl.multiple_of((p * 2 + c) * blk, LANES), blk), :]

    packs = kernel_call(pack_body, [shape((tok, width + vdim), bf16)] * (chips - 1), [both], "pack")
    weight_then, *packs = barrier((value_weight, *packs))
    (own_slice,) = kernel_call(slice_body, [shape((blk, vdim), bf16)], [weight_then], "own_slice")
    got = [across(x, q) for q, x in enumerate(packs, 1)]

    slots = sorted(range(1, n_tensor), key=lambda j: (j.bit_count(), -j))
    by_slot = {0: own_slice}
    for j in slots:
        by_slot[j] = along(by_slot[j & (j - 1)], j & -j)
    held = [by_slot[j] for j in slots]

    def quarter_body(act, cot, w, acc, grad, columns, sem):
        _, _, t = place()
        own = pl.ds(pl.multiple_of(t * quarter, LANES), quarter)
        columns[...] = contract(cot[...], w[...], 1, 1).astype(bf16)
        copy = pltpu.make_async_copy(columns, grad.at[:, own], sem)
        copy.start()
        acc[...] = contract(act[:, own], w[...], 1, 0)
        copy.wait()

    weight_then, _ = barrier((value_weight, held[0]))
    acc, grad = pl.pallas_call(
        quarter_body,
        out_shape=[shape((tok, vdim), f32), shape((tok, depth), bf16)],
        in_specs=[whole] * 3,
        out_specs=[whole, anywhere],
        scratch_shapes=[pltpu.VMEM((tok, quarter), bf16), pltpu.SemaphoreType.DMA],
        compiler_params=pltpu.CompilerParams(vmem_limit_bytes=VMEM_LIMIT),
        cost_estimate=estimate(0),
        name="own_quarter",
    )(activations, value_cotangent, weight_then)

    def sums_of(js_now, offset, cost):
        def body(act, cot, *refs):
            keep, send = refs[-2:]
            p, c, t = place()
            cots = jnp.concatenate([cot[...]] + [r[:, width:] for r in refs[:-2]], axis=0)
            for i, j in enumerate(js_now):
                for out, core in ((send, 1 - c), (keep, c)):
                    start = pl.multiple_of((offset + i) * 2 * blk + core * blk, LANES)
                    parts = [act[:, pl.ds(column(t ^ j, p, core), blk)]] + [r[:, pl.ds(start, blk)] for r in refs[:-2]]
                    out[i * blk : (i + 1) * blk, :] = contract(jnp.concatenate(parts, axis=0), cots, 0, 0)

        out = shape((len(js_now) * blk, vdim), f32)
        return kernel_call(body, [out, out], [activations, value_cotangent, *got], "sums", cost)

    def join(groups, pack, cost, after=()):
        arrays = []
        for group in groups:
            arrays += [a for a, _, _ in group if not any(a is b for b in arrays)]
        found = [[([a is b for b in arrays].index(True), at, power_at) for a, at, power_at in g] for g in groups]
        rows = len(groups) * blk

        def body(*refs):
            out = refs[-1]

            def value(k, at, power_at):
                x = refs[k][at : at + blk, :]
                return x if power_at is None else x * jnp.exp2(refs[k][power_at : power_at + 1, :])

            totals = []
            for g in found:
                total = value(*g[0])
                for term in g[1:]:
                    total = total + value(*term)
                totals.append(total)
            total = jnp.concatenate(totals, axis=0)
            if not pack:
                out[...] = total
                return
            top = jnp.max(jnp.abs(total), axis=(0, 1), keepdims=True)
            power = jnp.clip(jnp.ceil(jnp.log(jnp.maximum(top, 1e-30)) * LOG2_E) - TOP_POWER, -110.0, 110.0)
            out[:rows, :] = total * jnp.exp2(-power)
            out[rows:, :] = jnp.broadcast_to(power, (PAD, vdim))

        (out,) = kernel_call(body, [shape((rows + PAD if pack else rows, vdim), f32)], [*arrays, *after], "join", cost)
        return out.astype(jnp.float16) if pack else out

    got[0], acc, *_ = barrier((got[0], acc, *held))
    keep_1, send_1 = sums_of(js[:half], 0, 30)
    keep_2, send_2 = sums_of(js[half:], half, 20)
    mine = stack(held)
    twin_1, twin_2 = twin(send_1), twin(send_2)
    terms = {j: [(keep_1, i * blk, None), (twin_1, i * blk, None)] for i, j in enumerate(js[:half])}
    terms.update({j: [(keep_2, i * blk, None), (twin_2, i * blk, None)] for i, j in enumerate(js[half:])})

    rows = (n_tensor - 1) * blk
    singles = [1 << b for b in range(chips.bit_length() - 1)]
    late = [q for q in range(chips) if q.bit_count() >= 2]
    pieces = {0: [mine], **{q: [across(mine, q)] for q in singles}}

    def product(acc, grad, qs, ours, twins, total=None):
        last = total is not None
        n = (n_tensor - 1) * len(qs)

        def body(act, cot, acc, _, mine, twins, *refs):
            both = mine, twins
            p, c, t = place()
            if last:
                total, proj, grad, weight_grad, proj_out, grad_out, columns, sems = refs
                grad_out[...] = total[...] * (1.0 / root)
                copies = [pltpu.make_async_copy(grad_out, weight_grad, sems.at[n + 1])]
                copies[0].start()
            else:
                out, grad, columns, sems = refs
                copies = []
            order = [(at_q * (n_tensor - 1) + i, q, j, core) for at_q, q in enumerate(qs) for i, j in enumerate(slots) for core in range(2)]
            weights = [both[k][at * blk : (at + 1) * blk, :] for at, _, _, k in order]
            columns_of = [pl.ds(column(t ^ j, p ^ q, (c, 1 - c)[k]), blk) for _, q, j, k in order]
            lhs = jnp.concatenate([act[:, cols] for cols in columns_of], axis=1)
            result = acc[...] + contract(lhs, jnp.concatenate(weights, axis=0), 1, 0)
            if last:
                proj_out[...] = result.astype(bf16)
                copies.append(pltpu.make_async_copy(proj_out, proj, sems.at[n]))
                copies[-1].start()
            else:
                out[...] = result
            for (at, q, j, k), w in zip(order, weights):
                cols = pl.ds(pl.multiple_of((c, 1 - c)[k] * blk, LANES), blk)
                columns[at, :, cols] = contract(cot[...], w, 1, 1).astype(bf16)
                if k:
                    copies.append(pltpu.make_async_copy(columns.at[at], grad.at[:, pl.ds(column(t ^ j, p ^ q), 2 * blk)], sems.at[at]))
                    copies[-1].start()
            for copy in copies:
                copy.wait()

        args = [activations, value_cotangent, acc, grad, ours, twins] + [total] * last
        outs = [shape((tok, vdim), bf16 if last else f32), shape((tok, depth), bf16)] + [shape((blk, vdim), f32)] * last
        scratch = [pltpu.VMEM((tok, vdim), bf16), pltpu.VMEM((blk, vdim), f32)] * last
        return pl.pallas_call(
            body,
            out_shape=outs,
            in_specs=[whole] * 3 + [anywhere] + [whole] * (2 + last),
            out_specs=[anywhere] * 3 if last else [whole, anywhere],
            scratch_shapes=scratch + [pltpu.VMEM((n, tok, 2 * blk), bf16), pltpu.SemaphoreType.DMA((n + 2,))],
            input_output_aliases={3: 1},
            compiler_params=pltpu.CompilerParams(vmem_limit_bytes=VMEM_LIMIT),
            cost_estimate=estimate(0),
            name="product",
        )(*args)

    def tie(j, x):
        (a, at, power_at), *others = terms[j]
        a, x = barrier((a, x))
        terms[j] = [(a, at, power_at), *others]
        return x

    early, ours_early = [0, *singles], None
    for i, j in enumerate(js[:-1]):
        if i == half:
            ours_early = tie(j, stack([x for q in early for x in pieces[q]], 60))
            twin_early = twin(ours_early)
        if i > half:
            twin_early = tie(j, twin_early)
        packed = join([terms[j]], True, 30 if i == half else 0)
        if i == 0:
            _, *then = barrier((packed, *[pieces[q][0] for q in singles]))
            pieces.update({q: [x] for q, x in zip(singles, then)})
        arrived = along(packed, j & -j).astype(f32)
        terms[j & (j - 1)].append((arrived, 0, blk))
    if ours_early is None:
        ours_early = stack([x for q in early for x in pieces[q]], 60)
        twin_early = twin(ours_early)
    if not late:
        return product(acc, grad, early, ours_early, twin_early, join([terms[0]], False, 5))
    acc, grad = product(acc, grad, early, ours_early, twin_early)

    total = join([terms[0]], False, 5, [twin(acc[:8, :LANES])])
    for q in sorted(late, key=lambda q: q.bit_count()):
        bits = [b for b in singles if q & b]
        cuts = [rows * i // len(bits) // 16 * 16 for i in range(len(bits))] + [rows]
        ways = []
        for i, b in enumerate(bits):
            there = stack(pieces[q ^ b]) if len(pieces[q ^ b]) > 1 else pieces[q ^ b][0]
            ways.append(across(there[cuts[i] : cuts[i + 1]], b))
        pieces[q] = ways
    ours_late = stack([x for q in late for x in pieces[q]])
    return product(acc, grad, late, ours_late, twin(ours_late), total)


def solution(mesh):
    n_dp, n_tensor = mesh.shape["dp"], mesh.shape["tensor"]

    def per_device(activations, value_weight, value_cotangent):
        tok, depth = activations.shape
        powers = all(n > 1 and n & (n - 1) == 0 for n in (n_dp, n_tensor))
        if powers and depth % (n_dp * n_tensor * LANES) == 0 and tok % LANES == 0:
            return paired_form(n_dp, n_tensor, activations, value_weight, value_cotangent)
        return gathered_form(activations, value_weight, value_cotangent)

    return jax.shard_map(
        per_device,
        mesh=mesh,
        in_specs=(P(AXES, None), P("tensor", None), P(AXES, None)),
        out_specs=(P(AXES, None), P(AXES, None), P(("tensor", "dp"), None)),
        check_vma=False,
    )
```
